32 devices in a mesh: dp: 8 (over y, x, core), pipe: 4 (over z).
Axes of the slice: x: 2, y: 2, z: 4, core: 2. Of those that a mesh axis runs over, the one named last changes fastest.
Arguments:
- queries: bfloat16 [4, 1920, 2560], P('pipe', 'dp'), may hold values from -6 to 6
- key_rows: bfloat16 [4, 1920, 512], P('pipe', 'dp'), may hold values from -6 to 6
- value_rows: bfloat16 [4, 1920, 512], P('pipe', 'dp'), may hold values from -6 to 6
- out_grad: bfloat16 [4, 1920, 2560], P('pipe', 'dp'), may hold values from -6 to 6
- log_norm: bfloat16 [4, 20, 1920], P('pipe', None, 'dp'), may hold values from 2.5 to 4.5
- row_delta: bfloat16 [4, 20, 1920], P('pipe', None, 'dp'), may hold values from -24 to 24
- cand_lengths: int32 [4, 8, 3], P('pipe', 'dp'), may hold values from 0 to 80, as said below
Outputs:
- up_q: bfloat16 [4, 1920, 2560], P('pipe', 'dp')
- up_k: bfloat16 [4, 1920, 512], P('pipe', 'dp')
- up_v: bfloat16 [4, 1920, 512], P('pipe', 'dp')
- bias_grad: float32 [4, 3072], P('pipe', 'dp')
- value_bias_grad: float32 [4, 512], P('pipe', 'dp')
The draws below stay inside these ranges and needn't reach their ends.
Inputs may be any that keep to these rules, and one draw needn't show every extreme that they name: `cand_lengths`: each block's candidates fill its slots from the front, zeros marking empty slots, and the first slot is never empty; nonzero lengths are 64 or more, and the lengths of one block sum to at most 240. For the blocks i and i + 4 of one section, the rows of one block's candidates that end within its first 160 rows plus the rows of the other block's candidates that end beyond them come to at most 160, both ways round.
All inputs are finite; a program needn't handle non-finite values.
Results may differ from the reference program's by a relative error of at most 0.0054.
Values may be sent and summed in bfloat16 or wider, within the bound.
A program may use at most 64 MiB of HBM per device.

```python
import math
import jax
import jax.numpy as jnp
from jax import lax

HEADS = 20
KV_HEADS = 4
HEAD_DIM = 128
CANDIDATES = 3
LONGEST = 80
SHORTEST = 64
HOME_ROWS = 240
DP_RANKS = 8
SECTIONS = 4
TOKENS = 1920


def draw_cand_lengths(key, part):
    half_ranks = DP_RANKS // 2
    subkeys = jax.random.split(key, 7)
    shape = (SECTIONS, half_ranks, CANDIDATES)
    slot_index = jnp.arange(CANDIDATES, dtype=jnp.int32)
    heavy = jax.random.randint(subkeys[0], shape, SHORTEST, LONGEST + 1)
    dropped = jax.random.randint(subkeys[1], (SECTIONS, half_ranks), 0, 4) == 0
    pick_section = jax.random.randint(subkeys[2], (), 0, SECTIONS)
    pick_pair = jax.random.randint(subkeys[3], (), 0, half_ranks)
    forced = (jnp.arange(SECTIONS)[:, None] == pick_section) & (jnp.arange(half_ranks)[None, :] == pick_pair)
    dropped = dropped & jnp.logical_not(forced)
    heavy = jnp.where(dropped[:, :, None] & (slot_index == CANDIDATES - 1), 0, heavy)
    heavy = jnp.where(forced[:, :, None], LONGEST, heavy)
    light = jax.random.randint(subkeys[4], shape, SHORTEST, LONGEST + 1)
    light = jnp.where(forced[:, :, None] & (slot_index == 0), LONGEST, light)
    two_light = jax.random.randint(subkeys[6], (SECTIONS, half_ranks), 0, 2) == 1
    light_count = jnp.where(dropped & two_light, 2, 1)
    light = jnp.where(slot_index[None, None, :] < light_count[:, :, None], light, 0)
    flipped = jax.random.randint(subkeys[5], (SECTIONS, half_ranks), 0, 2) == 1
    lower_half = jnp.where(flipped[:, :, None], light, heavy)
    upper_half = jnp.where(flipped[:, :, None], heavy, light)
    return jnp.concatenate([lower_half, upper_half], axis=1).astype(jnp.int32)


def steps_of(stream_key, dims, cuts, low, largest):
    loudness = 1.0
    for axis_at, shards_of in cuts:
        heights = jax.random.uniform(jax.random.fold_in(jax.random.fold_in(stream_key, 6), axis_at), (shards_of,), jnp.float32, low / len(cuts), largest / len(cuts))
        loudness = loudness * jnp.repeat(jnp.exp(heights), dims[axis_at] // shards_of).reshape((-1,) + (1,) * (len(dims) - 1 - axis_at))
    return loudness


def noise(own_key, shape, deviation, limit, cuts=(), kind=jnp.bfloat16):
    result = jax.random.normal(own_key, shape, jnp.float32) * deviation
    if len(cuts) > 0:
        result = steps_of(own_key, shape, cuts, -0.22, 0.18) * result
    return jnp.clip(result, min=-limit, max=limit).astype(kind)


def setup_inputs(seed: int = 0) -> dict:
    arg_keys = jax.random.split(jax.random.key(seed), 8)
    queries = noise(arg_keys[0], (SECTIONS, TOKENS, HEADS * HEAD_DIM), 1.0, 6.0, ((0, 4), (1, 8)))
    key_rows = noise(arg_keys[1], (SECTIONS, TOKENS, KV_HEADS * HEAD_DIM), 1.0, 6.0, ((0, 4), (1, 8)))
    value_rows = noise(arg_keys[2], (SECTIONS, TOKENS, KV_HEADS * HEAD_DIM), 1.0, 6.0, ((0, 4), (1, 8)))
    out_grad = noise(arg_keys[3], (SECTIONS, TOKENS, HEADS * HEAD_DIM), 1.0, 6.0, ((0, 4), (1, 8)))
    log_norm = jnp.clip(2.5 + 2.0 * jax.random.uniform(arg_keys[4], (SECTIONS, HEADS, TOKENS), jnp.float32) ** steps_of(arg_keys[4], (SECTIONS, HEADS, TOKENS), ((0, 4), (2, 8)), -0.2, 0.2), 2.5, 4.5).astype(jnp.bfloat16)
    row_delta = noise(arg_keys[5], (SECTIONS, HEADS, TOKENS), 4.0, 24.0, ((0, 4), (2, 8)))
    cand_lengths = draw_cand_lengths(jax.random.fold_in(arg_keys[7], 71), 0)
    return {"queries": queries, "key_rows": key_rows, "value_rows": value_rows, "out_grad": out_grad, "log_norm": log_norm, "row_delta": row_delta, "cand_lengths": cand_lengths}


def segment_mask(lengths, row_count):
    row_ends = jnp.cumsum(lengths)
    position = jnp.arange(row_count, dtype=jnp.int32)
    labels = lax.optimization_barrier(jnp.sum((position[:, None] >= row_ends[None, :]).astype(jnp.int32), axis=1))
    inside = position < row_ends[-1]
    return (labels[:, None] == labels[None, :]) & inside[:, None] & inside[None, :]

def device_backward(pieces):
    query_part, key_part, value_part, grad_part, norm_part, delta_part, length_part = pieces
    row_count = query_part.shape[0]
    per_group = HEADS // KV_HEADS
    factor = 1.0 / math.sqrt(HEAD_DIM)
    allowed = segment_mask(length_part, row_count)
    query_heads = query_part.reshape(row_count, KV_HEADS, per_group, HEAD_DIM).astype(jnp.float32)
    grad_heads = grad_part.reshape(row_count, KV_HEADS, per_group, HEAD_DIM).astype(jnp.float32)
    key_heads = key_part.reshape(row_count, KV_HEADS, HEAD_DIM).astype(jnp.float32)
    value_heads = value_part.reshape(row_count, KV_HEADS, HEAD_DIM).astype(jnp.float32)
    norm_heads = norm_part.astype(jnp.float32).reshape(KV_HEADS, per_group, row_count)
    delta_heads = delta_part.astype(jnp.float32).reshape(KV_HEADS, per_group, row_count)
    scores = jnp.einsum('ikgd,jkd->kgij', query_heads, key_heads) * factor
    probs = jnp.where(allowed[None, None], jnp.exp(scores - norm_heads[..., None]), 0.0)
    dprobs = jnp.einsum('ikgd,jkd->kgij', grad_heads, value_heads)
    dscores = probs * (dprobs - delta_heads[..., None])
    probs_low = lax.optimization_barrier(probs.astype(jnp.bfloat16)).astype(jnp.float32)
    dscores_low = lax.optimization_barrier(dscores.astype(jnp.bfloat16)).astype(jnp.float32)
    grad_q = (jnp.einsum('kgij,jkd->ikgd', dscores_low, key_heads) * factor).astype(jnp.bfloat16)
    grad_k = (jnp.einsum('kgij,ikgd->jkd', dscores_low, query_heads) * factor).astype(jnp.bfloat16)
    grad_v = jnp.einsum('kgij,ikgd->jkd', probs_low, grad_heads).astype(jnp.bfloat16)
    return (grad_q.reshape(row_count, HEADS * HEAD_DIM), grad_k.reshape(row_count, KV_HEADS * HEAD_DIM), grad_v.reshape(row_count, KV_HEADS * HEAD_DIM))

def reference(queries, key_rows, value_rows, out_grad, log_norm, row_delta, cand_lengths):
    block_count = SECTIONS * DP_RANKS

    def rows_view(tensor):
        return tensor.reshape(block_count, HOME_ROWS, tensor.shape[-1])

    def head_view(tensor):
        split_view = tensor.reshape(SECTIONS, HEADS, DP_RANKS, HOME_ROWS)
        return jnp.moveaxis(split_view, 2, 1).reshape(block_count, HEADS, HOME_ROWS)
    grad_q, grad_k, grad_v = lax.map(device_backward, (rows_view(queries), rows_view(key_rows), rows_view(value_rows), rows_view(out_grad), head_view(log_norm), head_view(row_delta), cand_lengths.reshape(block_count, CANDIDATES)))
    grad_q = grad_q.reshape(SECTIONS, TOKENS, HEADS * HEAD_DIM)
    grad_k = grad_k.reshape(SECTIONS, TOKENS, KV_HEADS * HEAD_DIM)
    grad_v = grad_v.reshape(SECTIONS, TOKENS, KV_HEADS * HEAD_DIM)
    up_q = jnp.roll(grad_q, -1, axis=0)
    up_k = jnp.roll(grad_k, -1, axis=0)
    up_v = jnp.roll(grad_v, -1, axis=0)
    bias_grad = jnp.concatenate([lax.optimization_barrier(jnp.sum(up_q, axis=1, dtype=jnp.float32)), lax.optimization_barrier(jnp.sum(up_k, axis=1, dtype=jnp.float32))], axis=1)
    value_bias_grad = lax.optimization_barrier(jnp.sum(up_v, axis=1, dtype=jnp.float32))
    return (up_q, up_k, up_v, bias_grad, value_bias_grad)
```

```python
import functools
import math

import jax
import jax.numpy as jnp
from jax import lax
from jax.experimental import pallas as pl
from jax.experimental.pallas import tpu as pltpu
from jax.sharding import PartitionSpec as P

HEADS = 20
KV_HEADS = 4
HEAD_DIM = 128
PER_GROUP = HEADS // KV_HEADS
QUERY_WIDTH = PER_GROUP * HEAD_DIM
CHUNK = QUERY_WIDTH + 2 * HEAD_DIM
SLOT = 80
SLOTS = 3
FACTOR = 1.0 / math.sqrt(HEAD_DIM)
MESH = pl.DeviceIdType.MESH


def up_to_lanes(width):
    return -(-width // 128) * 128


def dot(a, b, dims):
    return lax.dot_general(a, b, (dims, ((), ())), preferred_element_type=jnp.float32)


def placement(lengths, rows, transposed):
    shape = (SLOTS * SLOT, rows) if not transposed else (rows, SLOTS * SLOT)
    slot_row = lax.broadcasted_iota(jnp.int32, shape, 1 if transposed else 0)
    row = lax.broadcasted_iota(jnp.int32, shape, 0 if transposed else 1)
    found = jnp.zeros(shape, jnp.float32)
    begin = jnp.zeros_like(lengths[0])
    for c in range(SLOTS):
        inside = slot_row - c * SLOT
        hit = (inside >= 0) & (inside < lengths[c]) & (row == inside + begin)
        found = jnp.where(hit, 1.0, found)
        begin = begin + lengths[c]
    return found.astype(jnp.bfloat16)


def kernel(
    dp, pipe, lengths_ref, q_ref, k_ref, v_ref, g_ref, norm_ref, delta_ref,
    up_q_ref, up_k_ref, up_v_ref, bias_ref, value_bias_ref,
    home_out, side_out, own_second, pair_out, home_in, side_in, pair_in, back_in,
    length_out, length_in, sums, sums_in, piece_out, piece_in,
    home_sem, side_sem, pair_sem, back_sem, length_sem, sums_sem, piece_sem,
):
    me, stage = lax.axis_index("dp"), lax.axis_index("pipe")
    before = {"dp": me, "pipe": (stage + pipe - 1) % pipe}
    after = {"dp": me, "pipe": (stage + 1) % pipe}
    steps = [1 << i for i in range(dp.bit_length() - 1)]

    def across(step):
        return {"dp": me + step - 2 * step * ((me // step) % 2), "pipe": stage}

    pair = across(dp // 2)
    barrier = pltpu.get_barrier_semaphore()
    greeted = [before, after] + [across(step) for step in steps]
    for device in greeted:
        pl.semaphore_signal(barrier, inc=1, device_id=device, device_id_type=MESH)
    pl.semaphore_wait(barrier, len(greeted))

    def remote(src, dst, sem, device):
        return pltpu.make_async_remote_copy(
            src_ref=src, dst_ref=dst, send_sem=sem.at[0], recv_sem=sem.at[1],
            device_id=device, device_id_type=MESH,
        )

    lengths = [lengths_ref[0, 0, c] for c in range(SLOTS)]
    line = lax.broadcasted_iota(jnp.int32, (8, 128), 0)
    length_out[...] = jnp.where(
        line == 0, lengths[0], jnp.where(line == 1, lengths[1], lengths[2])
    )
    length_copy = remote(length_out, length_in, length_sem, before)
    length_copy.start()

    rows = q_ref.shape[0]
    gather = placement(lengths, rows, False)
    norm_cols = dot(gather, norm_ref[...], ((1,), (1,)))
    delta_cols = dot(gather, delta_ref[...], ((1,), (1,)))
    column = lax.broadcasted_iota(jnp.int32, (PER_GROUP * SLOT, SLOT), 1)
    ones = jnp.ones((8, SLOTS * SLOT), jnp.bfloat16)

    home = [remote(home_out.at[g], home_in.at[g], home_sem.at[g], before) for g in range(KV_HEADS)]
    side = [remote(side_out.at[g], side_in.at[g], side_sem.at[g], before) for g in range(KV_HEADS)]
    lend = [remote(pair_out.at[g], pair_in.at[g], pair_sem.at[g], pair) for g in range(KV_HEADS)]
    back = [remote(side_in.at[g], back_in.at[g], back_sem.at[g], pair) for g in range(KV_HEADS)]

    def taken(ref, begin, width):
        return dot(gather, ref[:, begin : begin + width], ((1,), (0,))).astype(jnp.bfloat16)

    def send_side(g):
        lend[g].wait_recv()
        side_out[g] = own_second[g] + pair_in[g]
        side[g].start()

    for g in range(KV_HEADS):
        queries = taken(q_ref, g * QUERY_WIDTH, QUERY_WIDTH)
        grads = taken(g_ref, g * QUERY_WIDTH, QUERY_WIDTH)
        keys = taken(k_ref, g * HEAD_DIM, HEAD_DIM)
        values = taken(v_ref, g * HEAD_DIM, HEAD_DIM)
        for c in (2, 0, 1):
            at = slice(c * SLOT, (c + 1) * SLOT)
            heads = range(PER_GROUP)

            def stacked(x):
                return jnp.concatenate(
                    [x[at, h * HEAD_DIM : (h + 1) * HEAD_DIM] for h in heads], axis=0
                )

            def per_row(x):
                return jnp.concatenate(
                    [x[at, g * PER_GROUP + h : g * PER_GROUP + h + 1] for h in heads], axis=0
                )

            query, grad, key, value = stacked(queries), stacked(grads), keys[at], values[at]
            scores = dot(query, key, ((1,), (1,))) * FACTOR
            probs = jnp.where(column < lengths[c], jnp.exp(scores - per_row(norm_cols)), 0.0)
            dprobs = dot(grad, value, ((1,), (1,)))
            dscores = (probs * (dprobs - per_row(delta_cols))).astype(jnp.bfloat16)
            probs = probs.astype(jnp.bfloat16)
            grad_v = dot(probs, grad, ((0,), (0,))).astype(jnp.bfloat16)
            grad_k = (dot(dscores, query, ((0,), (0,))) * FACTOR).astype(jnp.bfloat16)
            grad_q = (dot(dscores, key, ((1,), (0,))) * FACTOR).astype(jnp.bfloat16)
            held = (home_out, own_second, pair_out)[c]
            for h in heads:
                held[g, :, h * HEAD_DIM : (h + 1) * HEAD_DIM] = grad_q[h * SLOT : (h + 1) * SLOT]
            held[g, :, QUERY_WIDTH : QUERY_WIDTH + HEAD_DIM] = grad_k
            held[g, :, QUERY_WIDTH + HEAD_DIM :] = grad_v
            if c == 2:
                lend[g].start()
            if c == 0:
                home[g].start()
        total = dot(
            ones,
            jnp.concatenate([home_out[g], own_second[g], pair_out[g]], axis=0),
            ((1,), (0,)),
        )[:1]
        sums[0, :, g * QUERY_WIDTH : (g + 1) * QUERY_WIDTH] = total[:, :QUERY_WIDTH]
        for i in range(2):
            begin = HEADS * HEAD_DIM + (i * KV_HEADS + g) * HEAD_DIM
            part = QUERY_WIDTH + i * HEAD_DIM
            sums[0, :, begin : begin + HEAD_DIM] = total[:, part : part + HEAD_DIM]
        if g > 0:
            send_side(g - 1)
    send_side(KV_HEADS - 1)

    exchanges = []
    for i, step in enumerate(steps):
        exchange = remote(sums.at[i], sums_in.at[i], sums_sem.at[i], across(step))
        exchange.start()
        exchange.wait_recv()
        sums[i + 1] = sums[i] + sums_in[i]
        exchanges.append(exchange)
    total = sums[len(steps)]
    width, value_width = bias_ref.shape[1], value_bias_ref.shape[1]
    value_at = up_to_lanes(width)
    value_from = (HEADS + KV_HEADS) * HEAD_DIM
    bias = jnp.zeros((1, width), jnp.float32)
    value_bias = jnp.zeros((1, value_width), jnp.float32)
    for j in range(dp):
        bias = jnp.where(me == j, total[:, j * width : (j + 1) * width], bias)
        value_begin = value_from + j * value_width
        value_bias = jnp.where(me == j, total[:, value_begin : value_begin + value_width], value_bias)
    piece_out[...] = jnp.zeros_like(piece_out)
    piece_out[:, :width] = bias
    piece_out[:, value_at : value_at + value_width] = value_bias
    piece_copy = remote(piece_out, piece_in, piece_sem, before)
    piece_copy.start()

    length_copy.wait_recv()
    scatter = placement([length_in[c : c + 1, :1] for c in range(SLOTS)], rows, True)
    for g in range(KV_HEADS):
        side[g].wait_recv()
        back[g].start()
    piece_copy.wait_recv()
    bias_ref[...] = piece_in[:, :width]
    value_bias_ref[...] = piece_in[:, value_at : value_at + value_width]
    for g in range(KV_HEADS):
        home[g].wait_recv()
        back[g].wait_recv()
        slots = jnp.concatenate([home_in[g], side_in[g], back_in[g]], axis=0)
        arrived = dot(scatter, slots, ((1,), (0,))).astype(jnp.bfloat16)
        up_q_ref[:, g * QUERY_WIDTH : (g + 1) * QUERY_WIDTH] = arrived[:, :QUERY_WIDTH]
        at = slice(g * HEAD_DIM, (g + 1) * HEAD_DIM)
        up_k_ref[:, at] = arrived[:, QUERY_WIDTH : QUERY_WIDTH + HEAD_DIM]
        up_v_ref[:, at] = arrived[:, QUERY_WIDTH + HEAD_DIM :]
    for copy in home + side + lend + back + exchanges + [length_copy, piece_copy]:
        copy.wait_send()


def solution(mesh):
    dp, pipe = mesh.shape["dp"], mesh.shape["pipe"]
    columns = (HEADS + 2 * KV_HEADS) * HEAD_DIM
    steps = dp.bit_length() - 1

    def shards(queries, key_rows, value_rows, out_grad, log_norm, row_delta, cand_lengths):
        rows = queries.shape[1]
        width = (HEADS + KV_HEADS) * HEAD_DIM // dp
        value_width = KV_HEADS * HEAD_DIM // dp
        piece = up_to_lanes(width) + up_to_lanes(value_width)
        chunk = pltpu.VMEM((KV_HEADS, SLOT, CHUNK), jnp.bfloat16)
        dma = pltpu.SemaphoreType.DMA
        vmem = pl.BlockSpec(memory_space=pltpu.VMEM)
        kv = jax.ShapeDtypeStruct((rows, KV_HEADS * HEAD_DIM), jnp.bfloat16)
        outs = pl.pallas_call(
            functools.partial(kernel, dp, pipe),
            out_shape=(
                jax.ShapeDtypeStruct((rows, HEADS * HEAD_DIM), jnp.bfloat16),
                kv,
                kv,
                jax.ShapeDtypeStruct((1, width), jnp.float32),
                jax.ShapeDtypeStruct((1, value_width), jnp.float32),
            ),
            in_specs=[pl.BlockSpec(memory_space=pltpu.SMEM)] + [vmem] * 6,
            out_specs=[vmem] * 5,
            scratch_shapes=[chunk] * 8
            + [
                pltpu.VMEM((8, 128), jnp.int32),
                pltpu.VMEM((8, 128), jnp.int32),
                pltpu.VMEM((steps + 1, 1, columns), jnp.float32),
                pltpu.VMEM((steps, 1, columns), jnp.float32),
                pltpu.VMEM((1, piece), jnp.float32),
                pltpu.VMEM((1, piece), jnp.float32),
            ]
            + [dma((KV_HEADS, 2))] * 4
            + [dma((2,)), dma((steps, 2)), dma((2,))],
            compiler_params=pltpu.CompilerParams(
                collective_id=0, has_side_effects=True, vmem_limit_bytes=40 * 2**20
            ),
        )(
            cand_lengths, queries[0], key_rows[0], value_rows[0], out_grad[0],
            log_norm[0], row_delta[0],
        )
        return (outs[0][None], outs[1][None], outs[2][None], outs[3], outs[4])

    rows = P("pipe", "dp", None)
    heads = P("pipe", None, "dp")
    sums = P("pipe", "dp")
    return jax.shard_map(
        shards,
        mesh=mesh,
        in_specs=(rows, rows, rows, rows, heads, heads, rows),
        out_specs=(rows, rows, rows, sums, sums),
        check_vma=False,
    )
```

```python
import functools
import math

import jax
import jax.numpy as jnp
from jax import lax
from jax.experimental import pallas as pl
from jax.experimental.pallas import tpu as pltpu
from jax.sharding import PartitionSpec as P

HEADS = 20
KV_HEADS = 4
HEAD_DIM = 128
PER_GROUP = HEADS // KV_HEADS
QUERY_WIDTH = PER_GROUP * HEAD_DIM
CHUNK = QUERY_WIDTH + 2 * HEAD_DIM
SLOT = 80
SLOTS = 3
FACTOR = 1.0 / math.sqrt(HEAD_DIM)
MESH = pl.DeviceIdType.MESH


def up_to_lanes(width):
    return -(-width // 128) * 128


def dot(a, b, dims):
    return lax.dot_general(a, b, (dims, ((), ())), preferred_element_type=jnp.float32)


def placement(lengths, rows, transposed):
    shape = (SLOTS * SLOT, rows) if not transposed else (rows, SLOTS * SLOT)
    slot_row = lax.broadcasted_iota(jnp.int32, shape, 1 if transposed else 0)
    row = lax.broadcasted_iota(jnp.int32, shape, 0 if transposed else 1)
    found = jnp.zeros(shape, jnp.float32)
    begin = jnp.zeros_like(lengths[0])
    for c in range(SLOTS):
        inside = slot_row - c * SLOT
        hit = (inside >= 0) & (inside < lengths[c]) & (row == inside + begin)
        found = jnp.where(hit, 1.0, found)
        begin = begin + lengths[c]
    return found.astype(jnp.bfloat16)


def kernel(
    dp, pipe, lengths_hbm, q_hbm, k_hbm, v_hbm, g_hbm, norm_hbm, delta_hbm,
    up_q_ref, up_k_ref, up_v_ref, bias_ref, value_bias_ref,
    lengths_ref, q_ref, k_ref, v_ref, g_ref, norm_ref, delta_ref, fetch_sem,
    home_out, side_out, own_second, pair_out, home_in, side_in, pair_in, back_in,
    length_out, length_in, sums, sums_in, piece_out, piece_in,
    home_sem, side_sem, pair_sem, back_sem, length_sem, sums_sem, piece_sem,
):
    fetched = [(lengths_hbm, lengths_ref), (norm_hbm, norm_ref), (delta_hbm, delta_ref)]
    fetched += [(k_hbm, k_ref), (v_hbm, v_ref)]
    for g in range(KV_HEADS):
        at = pl.ds(g * QUERY_WIDTH, QUERY_WIDTH)
        fetched += [(q_hbm.at[:, at], q_ref.at[:, at]), (g_hbm.at[:, at], g_ref.at[:, at])]
    fetches = [
        pltpu.make_async_copy(src, dst, fetch_sem.at[i]) for i, (src, dst) in enumerate(fetched)
    ]
    for fetch in fetches:
        fetch.start()

    me, stage = lax.axis_index("dp"), lax.axis_index("pipe")
    before = {"dp": me, "pipe": (stage + pipe - 1) % pipe}
    after = {"dp": me, "pipe": (stage + 1) % pipe}
    steps = [1 << i for i in range(dp.bit_length() - 1)]

    def across(step):
        return {"dp": me + step - 2 * step * ((me // step) % 2), "pipe": stage}

    pair = across(dp // 2)
    barrier = pltpu.get_barrier_semaphore()
    greeted = [before, after] + [across(step) for step in steps]
    for device in greeted:
        pl.semaphore_signal(barrier, inc=1, device_id=device, device_id_type=MESH)
    pl.semaphore_wait(barrier, len(greeted))

    def remote(src, dst, sem, device):
        return pltpu.make_async_remote_copy(
            src_ref=src, dst_ref=dst, send_sem=sem.at[0], recv_sem=sem.at[1],
            device_id=device, device_id_type=MESH,
        )

    for fetch in fetches[:3]:
        fetch.wait()
    lengths = [lengths_ref[0, 0, c] for c in range(SLOTS)]
    line = lax.broadcasted_iota(jnp.int32, (8, 128), 0)
    length_out[...] = jnp.where(
        line == 0, lengths[0], jnp.where(line == 1, lengths[1], lengths[2])
    )
    length_copy = remote(length_out, length_in, length_sem, before)
    length_copy.start()

    rows = q_ref.shape[0]
    gather = placement(lengths, rows, False)
    norm_cols = dot(gather, norm_ref[...], ((1,), (1,)))
    delta_cols = dot(gather, delta_ref[...], ((1,), (1,)))
    column = lax.broadcasted_iota(jnp.int32, (PER_GROUP * SLOT, SLOT), 1)
    ones = jnp.ones((8, SLOTS * SLOT), jnp.bfloat16)

    home = [remote(home_out.at[g], home_in.at[g], home_sem.at[g], before) for g in range(KV_HEADS)]
    side = [remote(side_out.at[g], side_in.at[g], side_sem.at[g], before) for g in range(KV_HEADS)]
    lend = [remote(pair_out.at[g], pair_in.at[g], pair_sem.at[g], pair) for g in range(KV_HEADS)]
    back = [remote(side_in.at[g], back_in.at[g], back_sem.at[g], pair) for g in range(KV_HEADS)]

    def taken(ref, begin, width):
        return dot(gather, ref[:, begin : begin + width], ((1,), (0,))).astype(jnp.bfloat16)

    early = KV_HEADS // 2

    def send_side(g):
        lend[g].wait_recv()
        side_out[g] = own_second[g] + pair_in[g]
        side[g].start()

    for fetch in fetches[3:5]:
        fetch.wait()
    for g in range(KV_HEADS):
        for fetch in fetches[5 + 2 * g : 7 + 2 * g]:
            fetch.wait()
        queries = taken(q_ref, g * QUERY_WIDTH, QUERY_WIDTH)
        grads = taken(g_ref, g * QUERY_WIDTH, QUERY_WIDTH)
        keys = taken(k_ref, g * HEAD_DIM, HEAD_DIM)
        values = taken(v_ref, g * HEAD_DIM, HEAD_DIM)
        for c in (2, 0, 1):
            at = slice(c * SLOT, (c + 1) * SLOT)
            heads = range(PER_GROUP)

            def stacked(x):
                return jnp.concatenate(
                    [x[at, h * HEAD_DIM : (h + 1) * HEAD_DIM] for h in heads], axis=0
                )

            def per_row(x):
                return jnp.concatenate(
                    [x[at, g * PER_GROUP + h : g * PER_GROUP + h + 1] for h in heads], axis=0
                )

            query, grad, key, value = stacked(queries), stacked(grads), keys[at], values[at]
            scores = dot(query, key, ((1,), (1,))) * FACTOR
            probs = jnp.where(column < lengths[c], jnp.exp(scores - per_row(norm_cols)), 0.0)
            dprobs = dot(grad, value, ((1,), (1,)))
            dscores = (probs * (dprobs - per_row(delta_cols))).astype(jnp.bfloat16)
            probs = probs.astype(jnp.bfloat16)
            grad_v = dot(probs, grad, ((0,), (0,))).astype(jnp.bfloat16)
            grad_k = (dot(dscores, query, ((0,), (0,))) * FACTOR).astype(jnp.bfloat16)
            grad_q = (dot(dscores, key, ((1,), (0,))) * FACTOR).astype(jnp.bfloat16)
            held = (home_out, own_second, pair_out)[c]
            for h in heads:
                held[g, :, h * HEAD_DIM : (h + 1) * HEAD_DIM] = grad_q[h * SLOT : (h + 1) * SLOT]
            held[g, :, QUERY_WIDTH : QUERY_WIDTH + HEAD_DIM] = grad_k
            held[g, :, QUERY_WIDTH + HEAD_DIM :] = grad_v
            if c == 2:
                lend[g].start()
            if c == 0 and g < early:
                home[g].start()
        total = dot(
            ones,
            jnp.concatenate([home_out[g], own_second[g], pair_out[g]], axis=0),
            ((1,), (0,)),
        )[:1]
        sums[0, :, g * QUERY_WIDTH : (g + 1) * QUERY_WIDTH] = total[:, :QUERY_WIDTH]
        for i in range(2):
            begin = HEADS * HEAD_DIM + (i * KV_HEADS + g) * HEAD_DIM
            part = QUERY_WIDTH + i * HEAD_DIM
            sums[0, :, begin : begin + HEAD_DIM] = total[:, part : part + HEAD_DIM]
        if g > 0:
            send_side(g - 1)
    exchanges = [
        remote(sums.at[i], sums_in.at[i], sums_sem.at[i], across(step))
        for i, step in enumerate(steps)
    ]
    exchanges[0].start()
    send_side(KV_HEADS - 1)
    home[early].start()
    for i in range(max(KV_HEADS, len(steps))):
        if i < KV_HEADS:
            side[i].wait_recv()
            back[i].start()
        if early + 1 + i < KV_HEADS:
            home[early + 1 + i].start()
        if i < len(steps):
            exchanges[i].wait_recv()
            sums[i + 1] = sums[i] + sums_in[i]
            if i + 1 < len(steps):
                exchanges[i + 1].start()
    total = sums[len(steps)]
    width, value_width = bias_ref.shape[1], value_bias_ref.shape[1]
    value_at = up_to_lanes(width)
    value_from = (HEADS + KV_HEADS) * HEAD_DIM
    bias = jnp.zeros((1, width), jnp.float32)
    value_bias = jnp.zeros((1, value_width), jnp.float32)
    for j in range(dp):
        bias = jnp.where(me == j, total[:, j * width : (j + 1) * width], bias)
        value_begin = value_from + j * value_width
        value_bias = jnp.where(me == j, total[:, value_begin : value_begin + value_width], value_bias)
    piece_out[...] = jnp.zeros_like(piece_out)
    piece_out[:, :width] = bias
    piece_out[:, value_at : value_at + value_width] = value_bias
    piece_copy = remote(piece_out, piece_in, piece_sem, before)
    piece_copy.start()

    length_copy.wait_recv()
    scatter = placement([length_in[c : c + 1, :1] for c in range(SLOTS)], rows, True)
    for g in range(KV_HEADS):
        home[g].wait_recv()
        back[g].wait_recv()
        slots = jnp.concatenate([home_in[g], side_in[g], back_in[g]], axis=0)
        arrived = dot(scatter, slots, ((1,), (0,))).astype(jnp.bfloat16)
        up_q_ref[:, g * QUERY_WIDTH : (g + 1) * QUERY_WIDTH] = arrived[:, :QUERY_WIDTH]
        at = slice(g * HEAD_DIM, (g + 1) * HEAD_DIM)
        up_k_ref[:, at] = arrived[:, QUERY_WIDTH : QUERY_WIDTH + HEAD_DIM]
        up_v_ref[:, at] = arrived[:, QUERY_WIDTH + HEAD_DIM :]
    piece_copy.wait_recv()
    bias_ref[...] = piece_in[:, :width]
    value_bias_ref[...] = piece_in[:, value_at : value_at + value_width]
    for copy in home + side + lend + back + exchanges + [length_copy, piece_copy]:
        copy.wait_send()


def written(*refs):
    count = len(refs) // 2
    sems = refs[-1]
    copies = [
        pltpu.make_async_copy(refs[i], refs[count + i], sems.at[i]) for i in range(count)
    ]
    for copy in copies:
        copy.start()
    for copy in copies:
        copy.wait()


def solution(mesh):
    dp, pipe = mesh.shape["dp"], mesh.shape["pipe"]
    columns = (HEADS + 2 * KV_HEADS) * HEAD_DIM
    steps = dp.bit_length() - 1

    def shards(queries, key_rows, value_rows, out_grad, log_norm, row_delta, cand_lengths):
        rows = queries.shape[1]
        width = (HEADS + KV_HEADS) * HEAD_DIM // dp
        value_width = KV_HEADS * HEAD_DIM // dp
        piece = up_to_lanes(width) + up_to_lanes(value_width)
        chunk = pltpu.VMEM((KV_HEADS, SLOT, CHUNK), jnp.bfloat16)
        dma = pltpu.SemaphoreType.DMA
        vmem = pl.BlockSpec(memory_space=pltpu.VMEM)
        kv = jax.ShapeDtypeStruct((rows, KV_HEADS * HEAD_DIM), jnp.bfloat16)
        hbm = pl.BlockSpec(memory_space=pltpu.HBM)
        shapes = (
            jax.ShapeDtypeStruct((rows, HEADS * HEAD_DIM), jnp.bfloat16),
            kv,
            kv,
            jax.ShapeDtypeStruct((1, width), jnp.float32),
            jax.ShapeDtypeStruct((1, value_width), jnp.float32),
        )
        operands = (
            cand_lengths, queries[0], key_rows[0], value_rows[0], out_grad[0],
            log_norm[0], row_delta[0],
        )
        outs = pl.pallas_call(
            functools.partial(kernel, dp, pipe),
            out_shape=shapes,
            in_specs=[hbm] * len(operands),
            out_specs=[vmem] * 5,
            scratch_shapes=[pltpu.SMEM(cand_lengths.shape, jnp.int32)]
            + [pltpu.VMEM(x.shape, x.dtype) for x in operands[1:]]
            + [dma((5 + 2 * KV_HEADS,))]
            + [chunk] * 8
            + [
                pltpu.VMEM((8, 128), jnp.int32),
                pltpu.VMEM((8, 128), jnp.int32),
                pltpu.VMEM((steps + 1, 1, columns), jnp.float32),
                pltpu.VMEM((steps, 1, columns), jnp.float32),
                pltpu.VMEM((1, piece), jnp.float32),
                pltpu.VMEM((1, piece), jnp.float32),
            ]
            + [dma((KV_HEADS, 2))] * 4
            + [dma((2,)), dma((steps, 2)), dma((2,))],
            compiler_params=pltpu.CompilerParams(
                collective_id=0, has_side_effects=True, vmem_limit_bytes=56 * 2**20
            ),
        )(*operands)
        outs = pl.pallas_call(
            written,
            out_shape=shapes,
            in_specs=[hbm] * 5,
            out_specs=[hbm] * 5,
            scratch_shapes=[dma((5,))],
            compiler_params=pltpu.CompilerParams(vmem_limit_bytes=56 * 2**20),
        )(*outs)
        return (outs[0][None], outs[1][None], outs[2][None], outs[3], outs[4])

    rows = P("pipe", "dp", None)
    heads = P("pipe", None, "dp")
    sums = P("pipe", "dp")
    return jax.shard_map(
        shards,
        mesh=mesh,
        in_specs=(rows, rows, rows, rows, heads, heads, rows),
        out_specs=(rows, rows, rows, sums, sums),
        check_vma=False,
    )
```

```python
import functools
import math

import jax
import jax.numpy as jnp
from jax import lax
from jax.experimental import pallas as pl
from jax.experimental.pallas import tpu as pltpu
from jax.sharding import PartitionSpec as P

HEADS = 20
KV_HEADS = 4
HEAD_DIM = 128
PER_GROUP = HEADS // KV_HEADS
QUERY_WIDTH = PER_GROUP * HEAD_DIM
CHUNK = QUERY_WIDTH + 2 * HEAD_DIM
SLOT = 80
SLOTS = 3
FACTOR = 1.0 / math.sqrt(HEAD_DIM)
MESH = pl.DeviceIdType.MESH


def up_to_lanes(width):
    return -(-width // 128) * 128


def dot(a, b, dims):
    return lax.dot_general(a, b, (dims, ((), ())), preferred_element_type=jnp.float32)


def placement(lengths, rows, transposed):
    shape = (SLOTS * SLOT, rows) if not transposed else (rows, SLOTS * SLOT)
    slot_row = lax.broadcasted_iota(jnp.int32, shape, 1 if transposed else 0)
    row = lax.broadcasted_iota(jnp.int32, shape, 0 if transposed else 1)
    found = jnp.zeros(shape, jnp.float32)
    begin = jnp.zeros_like(lengths[0])
    for c in range(SLOTS):
        inside = slot_row - c * SLOT
        hit = (inside >= 0) & (inside < lengths[c]) & (row == inside + begin)
        found = jnp.where(hit, 1.0, found)
        begin = begin + lengths[c]
    return found.astype(jnp.bfloat16)


def kernel(
    dp, pipe, lengths_hbm, q_hbm, k_hbm, v_hbm, g_hbm, norm_hbm, delta_hbm,
    up_q_ref, up_k_ref, up_v_ref, bias_ref, value_bias_ref,
    lengths_ref, q_ref, k_ref, v_ref, g_ref, norm_ref, delta_ref, fetch_sem,
    home_out, side_out, own_second, pair_out, home_in, side_in, pair_in, back_in,
    length_out, length_in, sums, sums_in, piece_out, piece_in,
    home_sem, side_sem, pair_sem, back_sem, length_sem, sums_sem, piece_sem,
):
    fetched = [(lengths_hbm, lengths_ref), (norm_hbm, norm_ref), (delta_hbm, delta_ref)]
    fetched += [(k_hbm, k_ref), (v_hbm, v_ref)]
    for g in range(KV_HEADS):
        at = pl.ds(g * QUERY_WIDTH, QUERY_WIDTH)
        fetched += [(q_hbm.at[:, at], q_ref.at[:, at]), (g_hbm.at[:, at], g_ref.at[:, at])]
    fetches = [
        pltpu.make_async_copy(src, dst, fetch_sem.at[i]) for i, (src, dst) in enumerate(fetched)
    ]
    for fetch in fetches:
        fetch.start()

    me, stage = lax.axis_index("dp"), lax.axis_index("pipe")
    before = {"dp": me, "pipe": (stage + pipe - 1) % pipe}
    after = {"dp": me, "pipe": (stage + 1) % pipe}
    steps = [1 << i for i in range(dp.bit_length() - 1)]

    def across(step):
        return {"dp": me + step - 2 * step * ((me // step) % 2), "pipe": stage}

    pair = across(dp // 2)
    barrier = pltpu.get_barrier_semaphore()
    greeted = [before, after] + [across(step) for step in steps]
    for device in greeted:
        pl.semaphore_signal(barrier, inc=1, device_id=device, device_id_type=MESH)
    pl.semaphore_wait(barrier, len(greeted))

    def remote(src, dst, sem, device):
        return pltpu.make_async_remote_copy(
            src_ref=src, dst_ref=dst, send_sem=sem.at[0], recv_sem=sem.at[1],
            device_id=device, device_id_type=MESH,
        )

    for fetch in fetches[:3]:
        fetch.wait()
    lengths = [lengths_ref[0, 0, c] for c in range(SLOTS)]
    line = lax.broadcasted_iota(jnp.int32, (8, 128), 0)
    length_out[...] = jnp.where(
        line == 0, lengths[0], jnp.where(line == 1, lengths[1], lengths[2])
    )
    length_copy = remote(length_out, length_in, length_sem, before)
    length_copy.start()

    rows = q_ref.shape[0]
    gather = placement(lengths, rows, False)
    norm_cols = dot(gather, norm_ref[...], ((1,), (1,)))
    delta_cols = dot(gather, delta_ref[...], ((1,), (1,)))
    column = lax.broadcasted_iota(jnp.int32, (PER_GROUP * SLOT, SLOT), 1)
    ones = jnp.ones((8, SLOTS * SLOT), jnp.bfloat16)

    home = [remote(home_out.at[g], home_in.at[g], home_sem.at[g], before) for g in range(KV_HEADS)]
    side = [remote(side_out.at[g], side_in.at[g], side_sem.at[g], before) for g in range(KV_HEADS)]
    lend = [remote(pair_out.at[g], pair_in.at[g], pair_sem.at[g], pair) for g in range(KV_HEADS)]
    back = [remote(side_in.at[g], back_in.at[g], back_sem.at[g], pair) for g in range(KV_HEADS)]

    def taken(ref, begin, width):
        return dot(gather, ref[:, begin : begin + width], ((1,), (0,))).astype(jnp.bfloat16)

    early = KV_HEADS // 2

    def send_side(g):
        lend[g].wait_recv()
        side_out[g] = own_second[g] + pair_in[g]
        side[g].start()

    for fetch in fetches[3:5]:
        fetch.wait()
    for g in range(KV_HEADS):
        for fetch in fetches[5 + 2 * g : 7 + 2 * g]:
            fetch.wait()
        queries = taken(q_ref, g * QUERY_WIDTH, QUERY_WIDTH)
        grads = taken(g_ref, g * QUERY_WIDTH, QUERY_WIDTH)
        keys = taken(k_ref, g * HEAD_DIM, HEAD_DIM)
        values = taken(v_ref, g * HEAD_DIM, HEAD_DIM)
        for c in (2, 0, 1):
            at = slice(c * SLOT, (c + 1) * SLOT)
            heads = range(PER_GROUP)

            def stacked(x):
                return jnp.concatenate(
                    [x[at, h * HEAD_DIM : (h + 1) * HEAD_DIM] for h in heads], axis=0
                )

            def per_row(x):
                return jnp.concatenate(
                    [x[at, g * PER_GROUP + h : g * PER_GROUP + h + 1] for h in heads], axis=0
                )

            query, grad, key, value = stacked(queries), stacked(grads), keys[at], values[at]
            scores = dot(query, key, ((1,), (1,))) * FACTOR
            probs = jnp.where(column < lengths[c], jnp.exp(scores - per_row(norm_cols)), 0.0)
            dprobs = dot(grad, value, ((1,), (1,)))
            dscores = (probs * (dprobs - per_row(delta_cols))).astype(jnp.bfloat16)
            probs = probs.astype(jnp.bfloat16)
            grad_v = dot(probs, grad, ((0,), (0,))).astype(jnp.bfloat16)
            grad_k = (dot(dscores, query, ((0,), (0,))) * FACTOR).astype(jnp.bfloat16)
            grad_q = (dot(dscores, key, ((1,), (0,))) * FACTOR).astype(jnp.bfloat16)
            held = (home_out, own_second, pair_out)[c]
            for h in heads:
                held[g, :, h * HEAD_DIM : (h + 1) * HEAD_DIM] = grad_q[h * SLOT : (h + 1) * SLOT]
            held[g, :, QUERY_WIDTH : QUERY_WIDTH + HEAD_DIM] = grad_k
            held[g, :, QUERY_WIDTH + HEAD_DIM :] = grad_v
            if c == 2:
                lend[g].start()
            if c == 0 and g < early:
                home[g].start()
        total = dot(
            ones,
            jnp.concatenate([home_out[g], own_second[g], pair_out[g]], axis=0),
            ((1,), (0,)),
        )[:1]
        sums[0, :, g * QUERY_WIDTH : (g + 1) * QUERY_WIDTH] = total[:, :QUERY_WIDTH]
        for i in range(2):
            begin = HEADS * HEAD_DIM + (i * KV_HEADS + g) * HEAD_DIM
            part = QUERY_WIDTH + i * HEAD_DIM
            sums[0, :, begin : begin + HEAD_DIM] = total[:, part : part + HEAD_DIM]
        if g > 0:
            send_side(g - 1)
    exchanges = [
        remote(sums.at[i], sums_in.at[i], sums_sem.at[i], across(step))
        for i, step in enumerate(steps)
    ]
    exchanges[0].start()
    send_side(KV_HEADS - 1)
    home[early].start()
    for i in range(max(KV_HEADS, len(steps))):
        if i < KV_HEADS:
            side[i].wait_recv()
            back[i].start()
        if early + 1 + i < KV_HEADS:
            home[early + 1 + i].start()
        if i < len(steps):
            exchanges[i].wait_recv()
            sums[i + 1] = sums[i] + sums_in[i]
            if i + 1 < len(steps):
                exchanges[i + 1].start()
    total = sums[len(steps)]
    width, value_width = bias_ref.shape[1], value_bias_ref.shape[1]
    value_at = up_to_lanes(width)
    value_from = (HEADS + KV_HEADS) * HEAD_DIM
    bias = jnp.zeros((1, width), jnp.float32)
    value_bias = jnp.zeros((1, value_width), jnp.float32)
    for j in range(dp):
        bias = jnp.where(me == j, total[:, j * width : (j + 1) * width], bias)
        value_begin = value_from + j * value_width
        value_bias = jnp.where(me == j, total[:, value_begin : value_begin + value_width], value_bias)
    piece_out[...] = jnp.zeros_like(piece_out)
    piece_out[:, :width] = bias
    piece_out[:, value_at : value_at + value_width] = value_bias
    piece_copy = remote(piece_out, piece_in, piece_sem, before)
    piece_copy.start()

    length_copy.wait_recv()
    scatter = placement([length_in[c : c + 1, :1] for c in range(SLOTS)], rows, True)
    for g in range(KV_HEADS):
        home[g].wait_recv()
        back[g].wait_recv()
        slots = jnp.concatenate([home_in[g], side_in[g], back_in[g]], axis=0)
        arrived = dot(scatter, slots, ((1,), (0,))).astype(jnp.bfloat16)
        up_q_ref[:, g * QUERY_WIDTH : (g + 1) * QUERY_WIDTH] = arrived[:, :QUERY_WIDTH]
        at = slice(g * HEAD_DIM, (g + 1) * HEAD_DIM)
        up_k_ref[:, at] = arrived[:, QUERY_WIDTH : QUERY_WIDTH + HEAD_DIM]
        up_v_ref[:, at] = arrived[:, QUERY_WIDTH + HEAD_DIM :]
    piece_copy.wait_recv()
    bias_ref[...] = piece_in[:, :width]
    value_bias_ref[...] = piece_in[:, value_at : value_at + value_width]
    for copy in home + side + lend + back + exchanges + [length_copy, piece_copy]:
        copy.wait_send()


def written(*refs):
    count = len(refs) // 2
    sems = refs[-1]
    copies = [
        pltpu.make_async_copy(refs[i], refs[count + i], sems.at[i]) for i in range(count)
    ]
    for copy in copies:
        copy.start()
    for copy in copies:
        copy.wait()


def solution(mesh):
    dp, pipe = mesh.shape["dp"], mesh.shape["pipe"]
    columns = (HEADS + 2 * KV_HEADS) * HEAD_DIM
    steps = dp.bit_length() - 1

    def shards(queries, key_rows, value_rows, out_grad, log_norm, row_delta, cand_lengths):
        rows = queries.shape[1]
        width = (HEADS + KV_HEADS) * HEAD_DIM // dp
        value_width = KV_HEADS * HEAD_DIM // dp
        piece = up_to_lanes(width) + up_to_lanes(value_width)
        chunk = pltpu.VMEM((KV_HEADS, SLOT, CHUNK), jnp.bfloat16)
        dma = pltpu.SemaphoreType.DMA
        vmem = pl.BlockSpec(memory_space=pltpu.VMEM)
        kv = jax.ShapeDtypeStruct((rows, KV_HEADS * HEAD_DIM), jnp.bfloat16)
        hbm = pl.BlockSpec(memory_space=pltpu.HBM)
        shapes = (
            jax.ShapeDtypeStruct((rows, HEADS * HEAD_DIM), jnp.bfloat16),
            kv,
            kv,
            jax.ShapeDtypeStruct((1, width), jnp.float32),
            jax.ShapeDtypeStruct((1, value_width), jnp.float32),
        )
        operands = (
            cand_lengths, queries[0], key_rows[0], value_rows[0], out_grad[0],
            log_norm[0], row_delta[0],
        )
        outs = pl.pallas_call(
            functools.partial(kernel, dp, pipe),
            out_shape=shapes,
            in_specs=[hbm] * len(operands),
            out_specs=[vmem] * 5,
            scratch_shapes=[pltpu.SMEM(cand_lengths.shape, jnp.int32)]
            + [pltpu.VMEM(x.shape, x.dtype) for x in operands[1:]]
            + [dma((5 + 2 * KV_HEADS,))]
            + [chunk] * 8
            + [
                pltpu.VMEM((8, 128), jnp.int32),
                pltpu.VMEM((8, 128), jnp.int32),
                pltpu.VMEM((steps + 1, 1, columns), jnp.float32),
                pltpu.VMEM((steps, 1, columns), jnp.float32),
                pltpu.VMEM((1, piece), jnp.float32),
                pltpu.VMEM((1, piece), jnp.float32),
            ]
            + [dma((KV_HEADS, 2))] * 4
            + [dma((2,)), dma((steps, 2)), dma((2,))],
            compiler_params=pltpu.CompilerParams(
                collective_id=0, has_side_effects=True, vmem_limit_bytes=40 * 2**20
            ),
        )(*[pltpu.with_memory_space_constraint(x, pltpu.HBM) for x in operands])
        outs = pl.pallas_call(
            written,
            out_shape=shapes,
            in_specs=[vmem] * 5,
            out_specs=[hbm] * 5,
            scratch_shapes=[dma((5,))],
            compiler_params=pltpu.CompilerParams(vmem_limit_bytes=16 * 2**20),
        )(*outs)
        return (outs[0][None], outs[1][None], outs[2][None], outs[3], outs[4])

    rows = P("pipe", "dp", None)
    heads = P("pipe", None, "dp")
    sums = P("pipe", "dp")
    return jax.shard_map(
        shards,
        mesh=mesh,
        in_specs=(rows, rows, rows, rows, heads, heads, rows),
        out_specs=(rows, rows, rows, sums, sums),
        check_vma=False,
    )
```

```python
import functools
import math

import jax
import jax.numpy as jnp
from jax import lax
from jax.experimental import pallas as pl
from jax.experimental.pallas import tpu as pltpu
from jax.sharding import PartitionSpec as P

HEADS = 20
KV_HEADS = 4
HEAD_DIM = 128
PER_GROUP = HEADS // KV_HEADS
QUERY_WIDTH = PER_GROUP * HEAD_DIM
CHUNK = QUERY_WIDTH + 2 * HEAD_DIM
SLOT = 80
SLOTS = 3
FACTOR = 1.0 / math.sqrt(HEAD_DIM)
MESH = pl.DeviceIdType.MESH


def up_to_lanes(width):
    return -(-width // 128) * 128


def dot(a, b, dims):
    return lax.dot_general(a, b, (dims, ((), ())), preferred_element_type=jnp.float32)


def placement(lengths, rows, transposed):
    shape = (SLOTS * SLOT, rows) if not transposed else (rows, SLOTS * SLOT)
    slot_row = lax.broadcasted_iota(jnp.int32, shape, 1 if transposed else 0)
    row = lax.broadcasted_iota(jnp.int32, shape, 0 if transposed else 1)
    found = jnp.zeros(shape, jnp.float32)
    begin = jnp.zeros_like(lengths[0])
    for c in range(SLOTS):
        inside = slot_row - c * SLOT
        hit = (inside >= 0) & (inside < lengths[c]) & (row == inside + begin)
        found = jnp.where(hit, 1.0, found)
        begin = begin + lengths[c]
    return found.astype(jnp.bfloat16)


def kernel(
    dp, pipe, lengths_hbm, q_hbm, k_hbm, v_hbm, g_hbm, norm_hbm, delta_hbm,
    up_q_ref, up_k_ref, up_v_ref, bias_ref, value_bias_ref,
    lengths_ref, q_ref, k_ref, v_ref, g_ref, norm_ref, delta_ref, fetch_sem,
    home_out, side_out, own_second, pair_out, home_in, side_in, pair_in, back_in,
    length_out, length_in, sums, sums_in, piece_out, piece_in,
    home_sem, side_sem, pair_sem, back_sem, length_sem, sums_sem, piece_sem,
):
    fetched = [(lengths_hbm, lengths_ref), (norm_hbm, norm_ref), (delta_hbm, delta_ref)]
    fetched += [(k_hbm, k_ref), (v_hbm, v_ref)]
    for g in range(KV_HEADS):
        at = pl.ds(g * QUERY_WIDTH, QUERY_WIDTH)
        fetched += [(q_hbm.at[:, at], q_ref.at[:, at]), (g_hbm.at[:, at], g_ref.at[:, at])]
    fetches = [
        pltpu.make_async_copy(src, dst, fetch_sem.at[i]) for i, (src, dst) in enumerate(fetched)
    ]
    for fetch in fetches:
        fetch.start()

    me, stage = lax.axis_index("dp"), lax.axis_index("pipe")
    before = {"dp": me, "pipe": (stage + pipe - 1) % pipe}
    after = {"dp": me, "pipe": (stage + 1) % pipe}
    steps = [1 << i for i in range(dp.bit_length() - 1)]

    def across(step):
        return {"dp": me + step - 2 * step * ((me // step) % 2), "pipe": stage}

    pair = across(dp // 2)
    barrier = pltpu.get_barrier_semaphore()
    greeted = [before, after] + [across(step) for step in steps]
    for device in greeted:
        pl.semaphore_signal(barrier, inc=1, device_id=device, device_id_type=MESH)
    pl.semaphore_wait(barrier, len(greeted))

    def remote(src, dst, sem, device):
        return pltpu.make_async_remote_copy(
            src_ref=src, dst_ref=dst, send_sem=sem.at[0], recv_sem=sem.at[1],
            device_id=device, device_id_type=MESH,
        )

    for fetch in fetches[:3]:
        fetch.wait()
    lengths = [lengths_ref[0, 0, c] for c in range(SLOTS)]
    line = lax.broadcasted_iota(jnp.int32, (8, 128), 0)
    length_out[...] = jnp.where(
        line == 0, lengths[0], jnp.where(line == 1, lengths[1], lengths[2])
    )
    length_copy = remote(length_out, length_in, length_sem, before)
    length_copy.start()

    rows = q_ref.shape[0]
    gather = placement(lengths, rows, False)
    norm_cols = dot(gather, norm_ref[...], ((1,), (1,)))
    delta_cols = dot(gather, delta_ref[...], ((1,), (1,)))
    column = lax.broadcasted_iota(jnp.int32, (PER_GROUP * SLOT, SLOT), 1)
    ones = jnp.ones((8, SLOTS * SLOT), jnp.bfloat16)

    home = [remote(home_out.at[g], home_in.at[g], home_sem.at[g], before) for g in range(KV_HEADS)]
    side = [remote(side_out.at[g], side_in.at[g], side_sem.at[g], before) for g in range(KV_HEADS)]
    lend = [remote(pair_out.at[g], pair_in.at[g], pair_sem.at[g], pair) for g in range(KV_HEADS)]
    back = [remote(side_in.at[g], back_in.at[g], back_sem.at[g], pair) for g in range(KV_HEADS)]

    def taken(ref, begin, width):
        return dot(gather, ref[:, begin : begin + width], ((1,), (0,))).astype(jnp.bfloat16)

    early = KV_HEADS // 2

    def send_side(g):
        lend[g].wait_recv()
        side_out[g] = own_second[g] + pair_in[g]
        side[g].start()

    for fetch in fetches[3:5]:
        fetch.wait()
    for g in range(KV_HEADS):
        for fetch in fetches[5 + 2 * g : 7 + 2 * g]:
            fetch.wait()
        queries = taken(q_ref, g * QUERY_WIDTH, QUERY_WIDTH)
        grads = taken(g_ref, g * QUERY_WIDTH, QUERY_WIDTH)
        keys = taken(k_ref, g * HEAD_DIM, HEAD_DIM)
        values = taken(v_ref, g * HEAD_DIM, HEAD_DIM)
        for c in (0, 2, 1) if g == 0 else (2, 0, 1):
            at = slice(c * SLOT, (c + 1) * SLOT)
            heads = range(PER_GROUP)

            def stacked(x):
                return jnp.concatenate(
                    [x[at, h * HEAD_DIM : (h + 1) * HEAD_DIM] for h in heads], axis=0
                )

            def per_row(x):
                return jnp.concatenate(
                    [x[at, g * PER_GROUP + h : g * PER_GROUP + h + 1] for h in heads], axis=0
                )

            query, grad, key, value = stacked(queries), stacked(grads), keys[at], values[at]
            scores = dot(query, key, ((1,), (1,))) * FACTOR
            probs = jnp.where(column < lengths[c], jnp.exp(scores - per_row(norm_cols)), 0.0)
            dprobs = dot(grad, value, ((1,), (1,)))
            dscores = (probs * (dprobs - per_row(delta_cols))).astype(jnp.bfloat16)
            probs = probs.astype(jnp.bfloat16)
            grad_v = dot(probs, grad, ((0,), (0,))).astype(jnp.bfloat16)
            grad_k = (dot(dscores, query, ((0,), (0,))) * FACTOR).astype(jnp.bfloat16)
            grad_q = (dot(dscores, key, ((1,), (0,))) * FACTOR).astype(jnp.bfloat16)
            held = (home_out, own_second, pair_out)[c]
            for h in heads:
                held[g, :, h * HEAD_DIM : (h + 1) * HEAD_DIM] = grad_q[h * SLOT : (h + 1) * SLOT]
            held[g, :, QUERY_WIDTH : QUERY_WIDTH + HEAD_DIM] = grad_k
            held[g, :, QUERY_WIDTH + HEAD_DIM :] = grad_v
            if c == 2:
                lend[g].start()
            if c == 0 and g < early:
                home[g].start()
        total = dot(
            ones,
            jnp.concatenate([home_out[g], own_second[g], pair_out[g]], axis=0),
            ((1,), (0,)),
        )[:1]
        sums[0, :, g * QUERY_WIDTH : (g + 1) * QUERY_WIDTH] = total[:, :QUERY_WIDTH]
        for i in range(2):
            begin = HEADS * HEAD_DIM + (i * KV_HEADS + g) * HEAD_DIM
            part = QUERY_WIDTH + i * HEAD_DIM
            sums[0, :, begin : begin + HEAD_DIM] = total[:, part : part + HEAD_DIM]
        if g > 0:
            send_side(g - 1)
    exchanges = [
        remote(sums.at[i], sums_in.at[i], sums_sem.at[i], across(step))
        for i, step in enumerate(steps)
    ]
    exchanges[0].start()
    send_side(KV_HEADS - 1)
    home[early].start()
    for i in range(max(KV_HEADS, len(steps))):
        if i < KV_HEADS:
            side[i].wait_recv()
            back[i].start()
        if early + 1 + i < KV_HEADS:
            home[early + 1 + i].start()
        if i < len(steps):
            exchanges[i].wait_recv()
            sums[i + 1] = sums[i] + sums_in[i]
            if i + 1 < len(steps):
                exchanges[i + 1].start()
    total = sums[len(steps)]
    width, value_width = bias_ref.shape[1], value_bias_ref.shape[1]
    value_at = up_to_lanes(width)
    value_from = (HEADS + KV_HEADS) * HEAD_DIM
    bias = jnp.zeros((1, width), jnp.float32)
    value_bias = jnp.zeros((1, value_width), jnp.float32)
    for j in range(dp):
        bias = jnp.where(me == j, total[:, j * width : (j + 1) * width], bias)
        value_begin = value_from + j * value_width
        value_bias = jnp.where(me == j, total[:, value_begin : value_begin + value_width], value_bias)
    piece_out[...] = jnp.zeros_like(piece_out)
    piece_out[:, :width] = bias
    piece_out[:, value_at : value_at + value_width] = value_bias
    piece_copy = remote(piece_out, piece_in, piece_sem, before)
    piece_copy.start()

    length_copy.wait_recv()
    scatter = placement([length_in[c : c + 1, :1] for c in range(SLOTS)], rows, True)
    for g in range(KV_HEADS):
        home[g].wait_recv()
        back[g].wait_recv()
        slots = jnp.concatenate([home_in[g], side_in[g], back_in[g]], axis=0)
        arrived = dot(scatter, slots, ((1,), (0,))).astype(jnp.bfloat16)
        up_q_ref[:, g * QUERY_WIDTH : (g + 1) * QUERY_WIDTH] = arrived[:, :QUERY_WIDTH]
        at = slice(g * HEAD_DIM, (g + 1) * HEAD_DIM)
        up_k_ref[:, at] = arrived[:, QUERY_WIDTH : QUERY_WIDTH + HEAD_DIM]
        up_v_ref[:, at] = arrived[:, QUERY_WIDTH + HEAD_DIM :]
    piece_copy.wait_recv()
    bias_ref[...] = piece_in[:, :width]
    value_bias_ref[...] = piece_in[:, value_at : value_at + value_width]
    for copy in home + side + lend + back + exchanges + [length_copy, piece_copy]:
        copy.wait_send()


def written(*refs):
    count = len(refs) // 2
    sems = refs[-1]
    copies = [
        pltpu.make_async_copy(refs[i], refs[count + i], sems.at[i]) for i in range(count)
    ]
    for copy in copies:
        copy.start()
    for copy in copies:
        copy.wait()


def solution(mesh):
    dp, pipe = mesh.shape["dp"], mesh.shape["pipe"]
    columns = (HEADS + 2 * KV_HEADS) * HEAD_DIM
    steps = dp.bit_length() - 1

    def shards(queries, key_rows, value_rows, out_grad, log_norm, row_delta, cand_lengths):
        rows = queries.shape[1]
        width = (HEADS + KV_HEADS) * HEAD_DIM // dp
        value_width = KV_HEADS * HEAD_DIM // dp
        piece = up_to_lanes(width) + up_to_lanes(value_width)
        chunk = pltpu.VMEM((KV_HEADS, SLOT, CHUNK), jnp.bfloat16)
        dma = pltpu.SemaphoreType.DMA
        vmem = pl.BlockSpec(memory_space=pltpu.VMEM)
        kv = jax.ShapeDtypeStruct((rows, KV_HEADS * HEAD_DIM), jnp.bfloat16)
        hbm = pl.BlockSpec(memory_space=pltpu.HBM)
        shapes = (
            jax.ShapeDtypeStruct((rows, HEADS * HEAD_DIM), jnp.bfloat16),
            kv,
            kv,
            jax.ShapeDtypeStruct((1, width), jnp.float32),
            jax.ShapeDtypeStruct((1, value_width), jnp.float32),
        )
        operands = (
            cand_lengths, queries[0], key_rows[0], value_rows[0], out_grad[0],
            log_norm[0], row_delta[0],
        )
        outs = pl.pallas_call(
            functools.partial(kernel, dp, pipe),
            out_shape=shapes,
            in_specs=[hbm] * len(operands),
            out_specs=[vmem] * 5,
            scratch_shapes=[pltpu.SMEM(cand_lengths.shape, jnp.int32)]
            + [pltpu.VMEM(x.shape, x.dtype) for x in operands[1:]]
            + [dma((5 + 2 * KV_HEADS,))]
            + [chunk] * 8
            + [
                pltpu.VMEM((8, 128), jnp.int32),
                pltpu.VMEM((8, 128), jnp.int32),
                pltpu.VMEM((steps + 1, 1, columns), jnp.float32),
                pltpu.VMEM((steps, 1, columns), jnp.float32),
                pltpu.VMEM((1, piece), jnp.float32),
                pltpu.VMEM((1, piece), jnp.float32),
            ]
            + [dma((KV_HEADS, 2))] * 4
            + [dma((2,)), dma((steps, 2)), dma((2,))],
            compiler_params=pltpu.CompilerParams(
                collective_id=0, has_side_effects=True, vmem_limit_bytes=40 * 2**20
            ),
        )(*[pltpu.with_memory_space_constraint(x, pltpu.HBM) for x in operands])
        outs = pl.pallas_call(
            written,
            out_shape=shapes,
            in_specs=[vmem] * 5,
            out_specs=[hbm] * 5,
            scratch_shapes=[dma((5,))],
            compiler_params=pltpu.CompilerParams(vmem_limit_bytes=16 * 2**20),
        )(*outs)
        return (outs[0][None], outs[1][None], outs[2][None], outs[3], outs[4])

    rows = P("pipe", "dp", None)
    heads = P("pipe", None, "dp")
    sums = P("pipe", "dp")
    return jax.shard_map(
        shards,
        mesh=mesh,
        in_specs=(rows, rows, rows, rows, heads, heads, rows),
        out_specs=(rows, rows, rows, sums, sums),
        check_vma=False,
    )
```
